512 devices in a mesh: ctx: 64 (over x, z_hi, y), tp: 8 (over z_lo, core).
Axes of the slice: x: 4, y: 4, z: 16 (z_hi: 4, z_lo: 4; z = z_hi * 4 + z_lo), core: 2. Of those that a mesh axis runs over, the one named last changes fastest.
Arguments:
- query_self: bfloat16 [8192, 8192], P('ctx', 'tp'), may hold values from -256 to 256
- key_value_self: bfloat16 [2, 8192, 1024], P(None, 'ctx', 'tp'), may hold values from -10 to 10
- query_cross: bfloat16 [8192, 8192], P('ctx', 'tp'), may hold values from -256 to 256
- panels: bfloat16 [2, 64, 64, 1024], P(None, 'ctx', 'tp'), may hold values from -10 to 10
- image_span: int32 [64, 2], replicated, may hold values from 0 to 8192, as said below
- panel_image: int32 [64], replicated, may hold values from 0 to 63, as said below
- cross_gate: float32 [1], replicated, may hold values from 0.5 to 2
Outputs:
- self_out: bfloat16 [8192, 8192], P('ctx', 'tp')
- cross_out: bfloat16 [8192, 8192], P('ctx', 'tp')
The draws below stay inside these ranges and needn't reach their ends.
Inputs may be any that keep to these rules, and one draw needn't show every extreme that they name: `image_span`: images come in groups of one to four consecutive images that share one range; the ranges of groups are disjoint, in order, and together cover all 8192 tokens; every image whose number is a multiple of 4 starts a group; image i (i > 0) opens its own range or lies in a group whose range begins at or before i * 128, and any range that begins with image i begins strictly inside tokens i * 128 to (i + 1) * 128 - 1, except image 0 at token 0; the last range ends at 8192. `panel_image`: each image is stored in exactly one slot, and slot p holds an image of the same aligned block of 4 slots (p // 4 equal).
All inputs are finite; a program needn't handle non-finite values.
Results may differ from the reference program's by a relative error of at most 0.0045.
Values may be sent and summed in bfloat16 or wider, within the bound.
A program may use at most 64 MiB of HBM per device.

```python
import jax
import jax.numpy as jnp
from jax import lax

QUERY_HEADS = 64
KEY_VALUE_HEADS = 8
HEAD_SIZE = 128
TOK_DEV = 128
IMAGE_TOKENS = 64
HEADS_PER_KEY = 8
TEXT_LENGTH = 8192
IMAGE_COUNT = 64


def spans(key):
    key = jax.random.fold_in(key, 7)
    index_list = jnp.arange(IMAGE_COUNT, dtype=jnp.int32)
    starts_new = jax.random.randint(jax.random.fold_in(key, 1), (IMAGE_COUNT,), 0, 5) < 2
    starts_new = starts_new | (index_list % 4 == 0)
    offsets = jax.random.randint(jax.random.fold_in(key, 2), (IMAGE_COUNT,), 1, TOK_DEV)
    marks_sorted = jnp.where(index_list == 0, 0, index_list * TOK_DEV + offsets).astype(jnp.int32)
    leaders = lax.cummax(jnp.where(starts_new, index_list, 0), axis=0)
    following = jnp.concatenate([jnp.where(starts_new, index_list, IMAGE_COUNT)[1:], jnp.array([IMAGE_COUNT], jnp.int32)])
    upcoming = lax.cummin(following, axis=0, reverse=True)
    opening = marks_sorted[leaders]
    closing = jnp.where(upcoming < IMAGE_COUNT, marks_sorted[jnp.minimum(upcoming, IMAGE_COUNT - 1)], TEXT_LENGTH)
    return jnp.stack([opening, closing], axis=1).astype(jnp.int32)


def owners(key):
    key = jax.random.fold_in(key, 5)
    index_list = jnp.arange(IMAGE_COUNT, dtype=jnp.int32)
    noise = jax.random.randint(key, (IMAGE_COUNT,), 0, 4096) * IMAGE_COUNT + index_list
    order_keys = index_list // 4 * (4096 * IMAGE_COUNT) + noise
    return jnp.argsort(order_keys, stable=True).astype(jnp.int32)


def paired_rows(start_offset):
    evens = start_offset[..., 0::2, :]
    odds = start_offset[..., 1::2, :]
    joined = jnp.stack([evens, odds], axis=-2)
    return joined.reshape(start_offset.shape)


def text_pairs(key):
    start_offset = jax.random.normal(jax.random.fold_in(key, 11), (2, TEXT_LENGTH, KEY_VALUE_HEADS * HEAD_SIZE), jnp.float32)
    return jnp.stack([paired_rows(start_offset[0].reshape(TEXT_LENGTH // 2 * 2, KEY_VALUE_HEADS * HEAD_SIZE)), start_offset[1]])


def panel_pairs(key):
    start_offset = jax.random.normal(jax.random.fold_in(key, 13), (2, IMAGE_COUNT, IMAGE_TOKENS, KEY_VALUE_HEADS * HEAD_SIZE), jnp.float32)
    return jnp.stack([paired_rows(start_offset[0]), start_offset[1]])


def draw_key_value_self(key, part):
    return text_pairs(key).astype(jnp.bfloat16)


def draw_query_self(key, part):
    key = jax.random.fold_in(key, 3)
    drawn = 3.0 * jax.random.normal(key, (TEXT_LENGTH, QUERY_HEADS * HEAD_SIZE), jnp.float32)
    return drawn.astype(jnp.bfloat16)


def draw_panels(key, part):
    return panel_pairs(key).astype(jnp.bfloat16)


def draw_image_span(key, part):
    return spans(key)


def draw_panel_image(key, part):
    return owners(key)


def draw_query_cross(key, part):
    key = jax.random.fold_in(key, 4)
    drawn = 3.0 * jax.random.normal(key, (TEXT_LENGTH, QUERY_HEADS * HEAD_SIZE), jnp.float32)
    return drawn.astype(jnp.bfloat16)


def setup_inputs(seed: int = 0) -> dict:
    streams_of = jax.random.split(jax.random.key(seed), 8)
    return {
        "query_self": draw_query_self(jax.random.fold_in(streams_of[7], 71), 0),
        "key_value_self": draw_key_value_self(jax.random.fold_in(streams_of[7], 71), 0),
        "query_cross": draw_query_cross(jax.random.fold_in(streams_of[7], 71), 0),
        "panels": draw_panels(jax.random.fold_in(streams_of[7], 71), 0),
        "image_span": draw_image_span(jax.random.fold_in(streams_of[7], 71), 0),
        "panel_image": draw_panel_image(jax.random.fold_in(streams_of[7], 71), 0),
        "cross_gate": jnp.clip(jax.random.uniform(streams_of[6], (1,), jnp.float32, 0.5, 2.0), 0.5, 2.0),
    }


NEG_FILL = -1e30


def attend(queries, key_row_block, value_rows, allowed):
    row_count, group_size, head_dim = queries.shape
    scores = jnp.dot(queries.reshape(row_count * group_size, head_dim), key_row_block.T, preferred_element_type=jnp.float32)
    scores = scores.reshape(row_count, group_size, -1) * (head_dim ** -0.5)
    visible = allowed[:, None, :]
    scores = jnp.where(visible, scores, NEG_FILL)
    maximum = jnp.max(scores, axis=2, keepdims=True)
    weights = jnp.where(visible, jnp.exp(scores - maximum), 0.0)
    totals = jnp.sum(weights, axis=2)
    summed = jnp.dot(weights.astype(jnp.bfloat16).reshape(row_count * group_size, -1), value_rows, preferred_element_type=jnp.float32)
    return summed.reshape(row_count, group_size, head_dim) / totals[:, :, None]


def reference(query_self, key_value_self, query_cross, panels, image_span, panel_image, cross_gate):
    block_length = 512 if TEXT_LENGTH % 512 == 0 else TEXT_LENGTH
    count_of_blocks = TEXT_LENGTH // block_length
    positions = jnp.arange(TEXT_LENGTH, dtype=jnp.int32)
    caption_queries = query_self.reshape(TEXT_LENGTH, KEY_VALUE_HEADS, HEADS_PER_KEY, HEAD_SIZE)
    vision_queries = query_cross.reshape(TEXT_LENGTH, KEY_VALUE_HEADS, HEADS_PER_KEY, HEAD_SIZE)
    caption_keys = key_value_self[0].reshape(TEXT_LENGTH, KEY_VALUE_HEADS, HEAD_SIZE)
    caption_values = key_value_self[1].reshape(TEXT_LENGTH, KEY_VALUE_HEADS, HEAD_SIZE)
    vision_keys = panels[0].reshape(IMAGE_COUNT * IMAGE_TOKENS, KEY_VALUE_HEADS, HEAD_SIZE)
    vision_values = panels[1].reshape(IMAGE_COUNT * IMAGE_TOKENS, KEY_VALUE_HEADS, HEAD_SIZE)
    image_ids = jnp.repeat(panel_image, IMAGE_TOKENS)
    opening = image_span[:, 0][image_ids]
    closing = image_span[:, 1][image_ids]
    zero = jnp.int32(0)

    def pick(which):
        kv_head = (which // count_of_blocks).astype(jnp.int32)
        block_index = (which % count_of_blocks).astype(jnp.int32)
        row_start = (block_index * block_length).astype(jnp.int32)
        query_pos = row_start + jnp.arange(block_length, dtype=jnp.int32)
        return kv_head, row_start, query_pos

    def self_block(which):
        kv_head, row_start, query_pos = pick(which)
        queries = lax.dynamic_slice(caption_queries, (row_start, kv_head, zero, zero), (block_length, 1, HEADS_PER_KEY, HEAD_SIZE))[:, 0]
        key_row_block = lax.dynamic_slice(caption_keys, (zero, kv_head, zero), (TEXT_LENGTH, 1, HEAD_SIZE))[:, 0]
        value_rows = lax.dynamic_slice(caption_values, (zero, kv_head, zero), (TEXT_LENGTH, 1, HEAD_SIZE))[:, 0]
        return attend(queries, key_row_block, value_rows, positions[None, :] <= query_pos[:, None])

    def cross_block(which):
        kv_head, row_start, query_pos = pick(which)
        queries = lax.dynamic_slice(vision_queries, (row_start, kv_head, zero, zero), (block_length, 1, HEADS_PER_KEY, HEAD_SIZE))[:, 0]
        key_row_block = lax.dynamic_slice(vision_keys, (zero, kv_head, zero), (IMAGE_COUNT * IMAGE_TOKENS, 1, HEAD_SIZE))[:, 0]
        value_rows = lax.dynamic_slice(vision_values, (zero, kv_head, zero), (IMAGE_COUNT * IMAGE_TOKENS, 1, HEAD_SIZE))[:, 0]
        allowed = (query_pos[:, None] >= opening[None, :]) & (query_pos[:, None] < closing[None, :])
        return attend(queries, key_row_block, value_rows, allowed)

    index_list = jnp.arange(KEY_VALUE_HEADS * count_of_blocks, dtype=jnp.int32)

    def assemble(block_list):
        reshaped_array = block_list.reshape(KEY_VALUE_HEADS, count_of_blocks, block_length, HEADS_PER_KEY, HEAD_SIZE)
        return reshaped_array.transpose(1, 2, 0, 3, 4).reshape(TEXT_LENGTH, QUERY_HEADS * HEAD_SIZE)

    self_out = assemble(lax.map(self_block, index_list)).astype(jnp.bfloat16)
    cross_out = (jnp.tanh(cross_gate[0]) * assemble(lax.map(cross_block, index_list))).astype(jnp.bfloat16)
    return (self_out, cross_out)
```

```python
import math

import jax
import jax.numpy as jnp
from jax import lax
from jax.experimental import pallas as pl
from jax.experimental.pallas import tpu as pltpu
from jax.sharding import PartitionSpec as P

MESH = pl.DeviceIdType.MESH
F32 = jnp.float32
BF16 = jnp.bfloat16
HEAD = 128
GROUP = 8
TOK = 128
COLS = GROUP * TOK
ROW = 4 * TOK
START = -1e30
HIDDEN = -1e38
EXPONENT = HEAD**-0.5 * math.log2(math.e)
NT = (((1,), (1,)), ((), ()))
ORIGIN = (0, 3, 1, 2)


def kernel(
    span, slot_image, gate, q_self, kv_own, q_cross, panels, self_out, cross_out,
    qs, kv, staged, pan, acc, top, tot, part_out, part_in, stat_out, stat_in,
    z_send, z_recv, x_send, x_recv, y_send, y_recv, r_send, r_recv,
    q_send, q_recv, o_send, o_recv, p_send, p_recv, s_send, s_recv,
):
    ctx = lax.axis_index("ctx")
    tp = lax.axis_index("tp")
    x, z, y = ctx // 16, (ctx // 4) % 4, ctx % 4
    bundle = ctx // 4

    def at(xx, zz, yy):
        return xx * 16 + zz * 4 + yy

    def origin(zi):
        if isinstance(zi, int):
            return (z + ORIGIN[zi]) % 4
        return (z + jnp.where(zi == 0, 0, jnp.where(zi == 1, 3, zi - 1))) % 4

    def remote(src, dst, send, recv, where):
        return pltpu.make_async_remote_copy(
            src_ref=src, dst_ref=dst, send_sem=send, recv_sem=recv, device_id=where, device_id_type=MESH
        )

    barrier = pltpu.get_barrier_semaphore()
    for d in (1, 2, 3):
        for peer in (at((x + d) % 4, z, y), at(x, (z + d) % 4, y), at(x, z, (y + d) % 4)):
            pl.semaphore_signal(barrier, inc=1, device_id=(peer, tp), device_id_type=MESH)
    for d in range(1, 8):
        pl.semaphore_signal(barrier, inc=1, device_id=(ctx, (tp + d) % 8), device_id_type=MESH)

    @pl.when((y == 0) & (bundle > 0))
    def _():
        for d in range(4):
            pl.semaphore_signal(barrier, inc=1, device_id=(ctx - 4 + d, tp), device_id_type=MESH)

    kv[0, ctx] = kv_own[0]
    kv[1, ctx] = kv_own[1]
    for h in range(GROUP):
        qs[0, pl.ds(h * TOK, TOK)] = q_self[:, h * HEAD : (h + 1) * HEAD]
    pair = jnp.concatenate([panels[0, 0].astype(F32), panels[1, 0].astype(F32)], axis=0)
    for h in range(GROUP):
        staged[h] = pair[:, h * HEAD : (h + 1) * HEAD].astype(BF16)

    pl.semaphore_wait(barrier, jnp.where(bundle < 15, 17, 16))

    def z_copy(kind, d):
        target = (z + {1: 1, 2: 3, 3: 2}[d]) % 4
        block = kv.at[kind, ctx]
        return remote(block, block, z_send.at[d, kind], z_recv.at[d, kind], (at(x, target, y), tp))

    def z_wait(kind, zi):
        block = kv.at[kind, at(x, origin(zi), y)]
        remote(block, block, z_send.at[0, 0], z_recv.at[zi, kind], (ctx, (tp + 1) % 8)).wait_recv()

    def item(i):
        if i < 2:
            return i, x
        if i == 2:
            return 0, x - 1
        return jnp.where(x == 3, 0, 1), jnp.where(x == 3, 1, x - 1)

    def y_copy(zi, i, way, yy):
        kind, plane = item(i)
        to = {0: (y + 1) % 4, 1: (y + 3) % 4, 2: (y + 2) % 4}[way]
        block = kv.at[kind, at(plane, origin(zi), yy)]
        return remote(block, block, y_send.at[zi, i, way], y_recv.at[zi, i, way], (at(x, z, to), tp))

    def y_onward(zi, i):
        kind, plane = item(i)
        up = i != 2
        from_y = (y + 3) % 4 if up else (y + 1) % 4
        to = (y + 1) % 4 if up else (y + 3) % 4
        block = kv.at[kind, at(plane, origin(zi), from_y)]
        return remote(block, block, y_send.at[zi, i, 2], y_recv.at[zi, i, 2], (at(x, z, to), tp))

    def y_wait(zi, i, way):
        kind, plane = item(i)
        yy = {0: (y + 3) % 4, 1: (y + 1) % 4, 2: (y + 2) % 4}[way]
        block = kv.at[kind, at(plane, origin(zi), yy)]
        remote(block, block, z_send.at[0, 0], y_recv.at[zi, i, way], (ctx, (tp + 1) % 8)).wait_recv()

    def x_copy(zi, kind, i, plane):
        block = kv.at[kind, at(x, origin(zi), y)]
        lane = 2 if plane is not None else kind
        to = x + 1 if plane is None else plane
        return remote(block, block, x_send.at[zi, lane], x_recv.at[zi, i], (at(to, z, y), tp))

    def x_wait(zi, i):
        kind, plane = item(i)
        block = kv.at[kind, at(plane, origin(zi), y)]
        remote(block, block, z_send.at[0, 0], x_recv.at[zi, i], (ctx, (tp + 1) % 8)).wait_recv()

    def row_copy(zi, plane, to, slot):
        rows = kv.at[1, pl.ds(at(plane, origin(zi), 0), 4)]
        return remote(rows, rows, r_send.at[zi], r_recv.at[zi, slot], (at(to, z, y), tp))

    def row_wait(zi, plane, slot):
        rows = kv.at[1, pl.ds(at(plane, origin(zi), 0), 4)]
        remote(rows, rows, z_send.at[0, 0], r_recv.at[zi, slot], (ctx, (tp + 1) % 8)).wait_recv()

    def q_copy():
        return remote(qs.at[0], qs.at[x - 1], q_send, q_recv.at[x - 1], (at(0, z, y), tp))

    def q_wait(slot):
        remote(qs.at[slot], qs.at[slot], q_send, q_recv.at[slot], (ctx, (tp + 1) % 8)).wait_recv()

    def o_copies(slot):
        to = (at(slot + 1, z, y), tp)
        return (
            remote(part_out.at[slot - 1], part_in, o_send.at[slot - 1, 0], o_recv.at[0], to),
            remote(stat_out.at[slot - 1], stat_in, o_send.at[slot - 1, 1], o_recv.at[1], to),
        )

    def p_copy(d):
        to = (tp + d) % 8
        return remote(staged.at[to], pan.at[y, tp], p_send.at[d], p_recv.at[d], (ctx, to))

    def p_wait(d):
        block = pan.at[y, (tp + 8 - d) % 8]
        remote(block, block, p_send.at[0], p_recv.at[d], (ctx, (tp + 1) % 8)).wait_recv()

    def s_copy(d):
        return remote(pan.at[y], pan.at[y], s_send.at[d], s_recv.at[d], (at(x, z, (y + d) % 4), tp))

    def s_wait(d):
        block = pan.at[(y + 4 - d) % 4]
        remote(block, block, s_send.at[d], s_recv.at[d], (ctx, (tp + 1) % 8)).wait_recv()

    def next_copy():
        return remote(pan.at[y], pan.at[4 + y], s_send.at[0], s_recv.at[4 + y], (ctx - y + 4, tp))

    def next_wait(d):
        block = pan.at[4 + d]
        remote(block, block, s_send.at[0], s_recv.at[4 + d], (ctx, (tp + 1) % 8)).wait_recv()

    def part1(zi):
        if not isinstance(zi, int) or zi > 0:
            z_wait(0, zi)

        @pl.when(x < 3)
        def _():
            x_copy(zi, 0, 2, None).start()

        @pl.when(x == 1)
        def _():
            x_copy(zi, 0, 3, 3).start()

        y_copy(zi, 0, 0, y).start()
        y_copy(zi, 0, 1, y).start()
        if not isinstance(zi, int) or zi > 0:
            z_wait(1, zi)

        @pl.when(x < 2)
        def _():
            x_copy(zi, 1, 3, None).start()

        for way in range(3):
            y_copy(zi, 1, way, y).start()

    def part2(zi):
        @pl.when(x > 0)
        def _():
            for i in (2, 3):
                x_wait(zi, i)
                y_copy(zi, i, 0, y).start()
                y_copy(zi, i, 1, y).start()

        y_wait(zi, 0, 0)
        y_onward(zi, 0).start()
        y_wait(zi, 0, 1)

    def part3(zi):
        for way in range(3):
            y_wait(zi, 1, way)

        @pl.when(x == 1)
        def _():
            row_copy(zi, 1, 0, 0).start()

        @pl.when(x == 2)
        def _():
            row_copy(zi, 2, 3, 0).start()

        @pl.when(x > 0)
        def _():
            for i in (2, 3):
                y_wait(zi, i, 0)
                if i == 3:
                    y_onward(zi, i).start()
                y_wait(zi, i, 1)
                if i == 2:
                    y_onward(zi, i).start()

    def part4(zi):
        @pl.when(x == 0)
        def _():
            row_wait(zi, 1, 0)
            row_copy(zi, 1, 3, 1).start()

    def reset(slot):
        acc[slot] = jnp.zeros((HEAD, COLS), F32)
        top[slot] = jnp.full((8, COLS), START, F32)
        tot[slot] = jnp.zeros((8, COLS), F32)

    def attend(slot, keys, values, hide):
        s = lax.dot_general(keys, qs[slot], NT, preferred_element_type=F32)
        s = hide(s)
        before = top[slot]
        now = jnp.maximum(before, jnp.max(s, axis=0, keepdims=True))
        p = jnp.exp2((s - now[:1]) * EXPONENT)
        scale = jnp.exp2((before - now) * EXPONENT)
        top[slot] = now
        tot[slot] = tot[slot] * scale + jnp.sum(p.reshape(-1, 8, COLS), axis=0)
        acc[slot] = acc[slot] * scale[:1] + jnp.dot(
            values.T, p.astype(BF16), preferred_element_type=F32
        )

    def row(kind, plane, zz):
        return kv[kind, pl.ds(at(plane, zz, 0), 4)].reshape(ROW, HEAD)

    token = lax.broadcasted_iota(jnp.int32, (1, COLS), 1) % TOK

    def attend_row(slot, plane, zz, causal):
        def hide(s):
            if not causal:
                return s
            key = at(plane, zz, 0) * TOK + lax.broadcasted_iota(jnp.int32, (ROW, COLS), 0)
            return jnp.where(key <= ctx * TOK + token, s, HIDDEN)

        attend(slot, row(0, plane, zz), row(1, plane, zz), hide)

    def attend_panels():
        reset(3)
        for h in range(GROUP):
            qs[3, pl.ds(h * TOK, TOK)] = q_cross[:, h * HEAD : (h + 1) * HEAD]
        for d in (1, 2, 3):
            s_wait(d)
        before = (y == 0) & (bundle > 0)

        @pl.when(before)
        def _():
            for d in range(4):
                next_wait(d)

        def half(which, _):
            block = pan[pl.ds(which * 4, 4)].reshape(32, 16, HEAD).astype(F32)
            keys = block[:, :8].reshape(256, HEAD).astype(BF16)
            values = block[:, 8:].reshape(256, HEAD).astype(BF16)
            here = ctx * TOK + token
            masks = []
            for k in range(4):
                image = slot_image[(bundle - which) * 4 + k]
                reads = (here >= span[image * 2]) & (here < span[image * 2 + 1])
                masks.append(jnp.broadcast_to(jnp.where(reads, 0.0, HIDDEN), (64, COLS)))
            mask = jnp.concatenate(masks, axis=0)
            attend(3, keys, values, lambda s: s + mask)
            return 0

        lax.fori_loop(0, jnp.where(before, 2, 1), half, 0)
        factor = jnp.tanh(jnp.full((1, COLS), gate[0], F32)) / jnp.sum(tot[3], axis=0, keepdims=True)
        for h in range(GROUP):
            c = slice(h * TOK, (h + 1) * TOK)
            cross_out[:, h * HEAD : (h + 1) * HEAD] = (acc[3, :, c] * factor[:, c]).T.astype(BF16)

    for kind in range(2):
        z_copy(kind, 1).start()
        z_copy(kind, 2).start()
    part1(0)
    for d in range(1, 8):
        p_copy(d).start()
    for kind in range(2):
        z_copy(kind, 3).start()

    @pl.when(x >= 2)
    def _():
        q_copy().start()

    pan[y, tp] = staged[tp]
    reset(0)

    @pl.when(x == 0)
    def _():
        reset(1)
        reset(2)

    part2(0)
    for d in range(1, 8):
        p_wait(d)
    for d in (1, 2, 3):
        s_copy(d).start()

    @pl.when(bundle < 15)
    def _():
        next_copy().start()

    part3(0)
    part1(1)

    def turn(zi, _):
        zz = origin(zi)

        @pl.when(zi < 3)
        def _():
            part2(zi + 1)

        y_wait(zi, 0, 2)

        @pl.when(zz <= z)
        def _():
            attend_row(0, x, zz, True)

        @pl.when(zi < 2)
        def _():
            part1(zi + 2)

        part4(zi)

        @pl.when(zi < 3)
        def _():
            part3(zi + 1)

        @pl.when(x > 0)
        def _():
            y_wait(zi, 2, 2)
            y_wait(zi, 3, 2)

        @pl.when(x == 3)
        def _():
            row_wait(zi, 2, 0)

        @pl.when((x == 0) & (zi == 0))
        def _():
            q_wait(1)
            q_wait(2)

        attend_row(jnp.where(x == 0, 1, 0), jnp.where(x == 0, 0, x - 1), zz, False)

        @pl.when(x == 3)
        def _():
            row_wait(zi, 1, 1)

        @pl.when((x == 0) | (x == 3))
        def _():
            attend_row(jnp.where(x == 0, 2, 0), jnp.where(x == 0, 0, 1), zz, False)

        @pl.when(zi == 0)
        def _():
            attend_panels()

        return 0

    lax.fori_loop(0, 4, turn, 0)

    @pl.when(x == 0)
    def _():
        upper = lax.broadcasted_iota(jnp.int32, (8, COLS), 0) < 4
        for slot in (1, 2):
            total = jnp.sum(tot[slot], axis=0, keepdims=True)
            part_out[slot - 1] = (acc[slot] * (1.0 / total)).astype(BF16)
            stat_out[slot - 1] = jnp.where(upper, top[slot], total)
            for copy in o_copies(slot):
                copy.start()

    @pl.when(x >= 2)
    def _():
        for copy in o_copies(1):
            copy.wait_recv()
        other_top, other_tot = stat_in[0:1], stat_in[4:5]
        own_top = top[0, 0:1]
        both = jnp.maximum(own_top, other_top)
        own = jnp.exp2((own_top - both) * EXPONENT)
        other = other_tot * jnp.exp2((other_top - both) * EXPONENT)
        acc[0] = acc[0] * own + part_in[...].astype(F32) * other
        first = lax.broadcasted_iota(jnp.int32, (8, COLS), 0) == 0
        tot[0] = tot[0] * own + jnp.where(first, other, 0.0)

    inverse = 1.0 / jnp.sum(tot[0], axis=0, keepdims=True)
    for h in range(GROUP):
        c = slice(h * TOK, (h + 1) * TOK)
        self_out[:, h * HEAD : (h + 1) * HEAD] = (acc[0, :, c] * inverse[:, c]).T.astype(BF16)

    for d in (1, 2, 3):
        for kind in range(2):
            z_copy(kind, d).wait_send()
        s_copy(d).wait_send()
    for d in range(1, 8):
        p_copy(d).wait_send()

    @pl.when(bundle < 15)
    def _():
        next_copy().wait_send()

    def drain(zi, _):
        for i in (0, 1):
            for way in range(3):
                y_copy(zi, i, way, y).wait_send()

        @pl.when(x > 0)
        def _():
            for i in (2, 3):
                for way in range(3):
                    y_copy(zi, i, way, y).wait_send()

        @pl.when(x < 3)
        def _():
            x_copy(zi, 0, 2, None).wait_send()
            row_copy(zi, 1, 3, 1).wait_send()

        @pl.when(x < 2)
        def _():
            x_copy(zi, 1, 3, None).wait_send()

        @pl.when(x == 1)
        def _():
            x_copy(zi, 0, 3, 3).wait_send()

        return 0

    lax.fori_loop(0, 4, drain, 0)

    @pl.when(x >= 2)
    def _():
        q_copy().wait_send()

    @pl.when(x == 0)
    def _():
        for slot in (1, 2):
            for copy in o_copies(slot):
                copy.wait_send()


def local(query_self, key_value_self, query_cross, panels, image_span, panel_image, cross_gate):
    smem = pl.BlockSpec(memory_space=pltpu.SMEM)
    vmem = pl.BlockSpec(memory_space=pltpu.VMEM)
    dma = pltpu.SemaphoreType.DMA
    shape = jax.ShapeDtypeStruct((TOK, COLS), BF16)
    return pl.pallas_call(
        kernel,
        out_shape=(shape, shape),
        in_specs=[smem] * 3 + [vmem] * 4,
        out_specs=(vmem, vmem),
        scratch_shapes=[
            pltpu.VMEM((4, COLS, HEAD), BF16),
            pltpu.VMEM((2, 64, TOK, HEAD), BF16),
            pltpu.VMEM((8, 16, HEAD), BF16),
            pltpu.VMEM((8, 8, 16, HEAD), BF16),
            pltpu.VMEM((4, HEAD, COLS), F32),
            pltpu.VMEM((4, 8, COLS), F32),
            pltpu.VMEM((4, 8, COLS), F32),
            pltpu.VMEM((2, HEAD, COLS), BF16),
            pltpu.VMEM((HEAD, COLS), BF16),
            pltpu.VMEM((2, 8, COLS), F32),
            pltpu.VMEM((8, COLS), F32),
            dma((4, 2)), dma((4, 2)),
            dma((4, 3)), dma((4, 4)),
            dma((4, 4, 3)), dma((4, 4, 3)),
            dma((4,)), dma((4, 2)),
            dma, dma((3,)),
            dma((2, 2)), dma((2,)),
            dma((8,)), dma((8,)),
            dma((4,)), dma((8,)),
        ],
        compiler_params=pltpu.CompilerParams(
            collective_id=0, has_side_effects=True, vmem_limit_bytes=48 << 20
        ),
        name="attention",
    )(image_span.reshape(-1), panel_image, cross_gate, query_self, key_value_self, query_cross, panels)


def solution(mesh):
    return jax.shard_map(
        local,
        mesh=mesh,
        in_specs=(
            P("ctx", "tp"),
            P(None, "ctx", "tp"),
            P("ctx", "tp"),
            P(None, "ctx", "tp", None),
            P(),
            P(),
            P(),
        ),
        out_specs=(P("ctx", "tp"), P("ctx", "tp")),
        check_vma=False,
    )
```

```python
import math

import jax
import jax.numpy as jnp
from jax import lax
from jax.experimental import pallas as pl
from jax.experimental.pallas import tpu as pltpu
from jax.sharding import PartitionSpec as P

MESH = pl.DeviceIdType.MESH
F32 = jnp.float32
BF16 = jnp.bfloat16
HEAD = 128
GROUP = 8
TOK = 128
COLS = GROUP * TOK
ROW = 4 * TOK
START = -1e30
HIDDEN = -1e38
EXPONENT = HEAD**-0.5 * math.log2(math.e)
NT = (((1,), (1,)), ((), ()))
ORIGIN = (0, 3, 1, 2)


def kernel(
    span, slot_image, gate, q_self, kv_own, q_cross, panels, self_out, cross_out,
    qs, kv, staged, pan, acc, top, tot, part_out, part_in, stat_out, stat_in,
    z_send, z_recv, x_send, x_recv, y_send, y_recv, r_send, r_recv,
    q_send, q_recv, o_send, o_recv, p_send, p_recv, s_send, s_recv, panel_in, in_sem,
):
    ctx = lax.axis_index("ctx")
    tp = lax.axis_index("tp")
    x, z, y = ctx // 16, (ctx // 4) % 4, ctx % 4
    bundle = ctx // 4

    def at(xx, zz, yy):
        return xx * 16 + zz * 4 + yy

    def origin(zi):
        if isinstance(zi, int):
            return (z + ORIGIN[zi]) % 4
        return (z + jnp.where(zi == 0, 0, jnp.where(zi == 1, 3, zi - 1))) % 4

    def remote(src, dst, send, recv, where):
        return pltpu.make_async_remote_copy(
            src_ref=src, dst_ref=dst, send_sem=send, recv_sem=recv, device_id=where, device_id_type=MESH
        )

    def reset(slot):
        acc[slot] = jnp.zeros((HEAD, COLS), F32)
        top[slot] = jnp.full((8, COLS), START, F32)
        tot[slot] = jnp.zeros((8, COLS), F32)

    barrier = pltpu.get_barrier_semaphore()
    for d in (1, 2, 3):
        for peer in (at((x + d) % 4, z, y), at(x, (z + d) % 4, y), at(x, z, (y + d) % 4)):
            pl.semaphore_signal(barrier, inc=1, device_id=(peer, tp), device_id_type=MESH)
    for d in range(1, 8):
        pl.semaphore_signal(barrier, inc=1, device_id=(ctx, (tp + d) % 8), device_id_type=MESH)

    @pl.when((y == 0) & (bundle > 0))
    def _():
        for d in range(4):
            pl.semaphore_signal(barrier, inc=1, device_id=(ctx - 4 + d, tp), device_id_type=MESH)

    own_kv = [pltpu.make_async_copy(kv_own.at[k], kv.at[k, ctx], in_sem.at[k]) for k in range(2)]
    own_panel = pltpu.make_async_copy(panels, panel_in, in_sem.at[2])

    def load_queries(array, slot, sem):
        return [
            pltpu.make_async_copy(
                array.at[:, pl.ds(h * HEAD, HEAD)], qs.at[slot, pl.ds(h * TOK, TOK)], in_sem.at[sem]
            )
            for h in range(GROUP)
        ]

    for copy in own_kv + [own_panel] + load_queries(q_self, 0, 3) + load_queries(q_cross, 3, 4):
        copy.start()

    def wait_queries(slot, sem):
        pltpu.make_async_copy(qs.at[slot], qs.at[slot], in_sem.at[sem]).wait()

    reset(0)

    @pl.when(x == 0)
    def _():
        reset(1)
        reset(2)

    own_panel.wait()
    pair = jnp.concatenate([panel_in[0, 0].astype(F32), panel_in[1, 0].astype(F32)], axis=0)
    for h in range(GROUP):
        staged[h] = pair[:, h * HEAD : (h + 1) * HEAD].astype(BF16)

    for copy in own_kv:
        copy.wait()
    pl.semaphore_wait(barrier, jnp.where(bundle < 15, 17, 16))

    def z_copy(kind, d):
        target = (z + {1: 1, 2: 3}[d]) % 4
        block = kv.at[kind, ctx]
        return remote(block, block, z_send.at[d, kind], z_recv.at[d, kind], (at(x, target, y), tp))

    def z_half(kind, zz, half):
        return kv.at[kind, at(x, zz, y), pl.ds(half * 64, 64)]

    def z_onward(kind, half):
        step = 3 if half == 0 else 1
        block = z_half(kind, (z + step) % 4, half)
        where = (at(x, (z + 4 - step) % 4, y), tp)
        return remote(block, block, z_send.at[3 * half, kind], z_recv.at[3 * half, kind], where)

    def z_wait(kind, zi):
        aside = (ctx, (tp + 1) % 8)
        if zi < 3:
            block = kv.at[kind, at(x, origin(zi), y)]
            remote(block, block, z_send.at[0, 0], z_recv.at[zi, kind], aside).wait_recv()
            return
        for half in range(2):
            block = z_half(kind, origin(3), half)
            remote(block, block, z_send.at[0, 0], z_recv.at[3 * half, kind], aside).wait_recv()

    def item(i):
        if i < 2:
            return i, x
        if i == 2:
            return 0, x - 1
        return jnp.where(x == 3, 0, 1), jnp.where(x == 3, 1, x - 1)

    def y_copy(zi, i, way, yy):
        kind, plane = item(i)
        to = {0: (y + 1) % 4, 1: (y + 3) % 4, 2: (y + 2) % 4}[way]
        block = kv.at[kind, at(plane, origin(zi), yy)]
        return remote(block, block, y_send.at[zi, i, way], y_recv.at[zi, i, way], (at(x, z, to), tp))

    def y_onward(zi, i):
        kind, plane = item(i)
        up = i != 2
        from_y = (y + 3) % 4 if up else (y + 1) % 4
        to = (y + 1) % 4 if up else (y + 3) % 4
        block = kv.at[kind, at(plane, origin(zi), from_y)]
        return remote(block, block, y_send.at[zi, i, 2], y_recv.at[zi, i, 2], (at(x, z, to), tp))

    def y_wait(zi, i, way):
        kind, plane = item(i)
        yy = {0: (y + 3) % 4, 1: (y + 1) % 4, 2: (y + 2) % 4}[way]
        block = kv.at[kind, at(plane, origin(zi), yy)]
        remote(block, block, z_send.at[0, 0], y_recv.at[zi, i, way], (ctx, (tp + 1) % 8)).wait_recv()

    def x_copy(zi, kind, i, plane):
        block = kv.at[kind, at(x, origin(zi), y)]
        lane = kind if plane is None else 2
        to = x + 1 if plane is None else plane
        return remote(block, block, x_send.at[zi, lane], x_recv.at[zi, i], (at(to, z, y), tp))

    def x_wait(zi, i):
        kind, plane = item(i)
        block = kv.at[kind, at(plane, origin(zi), y)]
        remote(block, block, z_send.at[0, 0], x_recv.at[zi, i], (ctx, (tp + 1) % 8)).wait_recv()

    def row_copy(zi):
        rows = kv.at[1, pl.ds(at(x, origin(zi), 0), 4)]
        return remote(rows, rows, r_send.at[zi], r_recv.at[zi, 2 - x], (at(3, z, y), tp))

    def row_wait(zi, plane, slot):
        rows = kv.at[1, pl.ds(at(plane, origin(zi), 0), 4)]
        remote(rows, rows, z_send.at[0, 0], r_recv.at[zi, slot], (ctx, (tp + 1) % 8)).wait_recv()

    def q_copy():
        return remote(qs.at[0], qs.at[x - 1], q_send, q_recv.at[x - 1], (at(0, z, y), tp))

    def q_wait(slot):
        remote(qs.at[slot], qs.at[slot], q_send, q_recv.at[slot], (ctx, (tp + 1) % 8)).wait_recv()

    def o_copies(slot):
        to = (at(slot + 1, z, y), tp)
        return (
            remote(part_out.at[slot - 1], part_in, o_send.at[slot - 1, 0], o_recv.at[0], to),
            remote(stat_out.at[slot - 1], stat_in, o_send.at[slot - 1, 1], o_recv.at[1], to),
        )

    def p_copy(d):
        to = (tp + d) % 8
        return remote(staged.at[to], pan.at[y, tp], p_send.at[d], p_recv.at[d], (ctx, to))

    def p_wait(d):
        block = pan.at[y, (tp + 8 - d) % 8]
        remote(block, block, p_send.at[0], p_recv.at[d], (ctx, (tp + 1) % 8)).wait_recv()

    def s_copy(d):
        return remote(pan.at[y], pan.at[y], s_send.at[d], s_recv.at[d], (at(x, z, (y + d) % 4), tp))

    def s_wait(d):
        block = pan.at[(y + 4 - d) % 4]
        remote(block, block, s_send.at[d], s_recv.at[d], (ctx, (tp + 1) % 8)).wait_recv()

    def next_copy():
        return remote(pan.at[y], pan.at[4 + y], s_send.at[0], s_recv.at[4 + y], (ctx - y + 4, tp))

    def next_wait(d):
        block = pan.at[4 + d]
        remote(block, block, s_send.at[0], s_recv.at[4 + d], (ctx, (tp + 1) % 8)).wait_recv()

    def keys_out(zi):
        if zi > 0:
            z_wait(0, zi)
        if zi in (1, 2):
            z_onward(0, zi - 1).start()

        @pl.when(x < 3)
        def _():
            x_copy(zi, 0, 2, None).start()

        @pl.when(x == 1)
        def _():
            x_copy(zi, 0, 3, 3).start()

        y_copy(zi, 0, 0, y).start()
        y_copy(zi, 0, 1, y).start()

    def values_out(zi):
        if zi > 0:
            z_wait(1, zi)
        if zi in (1, 2):
            z_onward(1, zi - 1).start()

        @pl.when(x < 2)
        def _():
            x_copy(zi, 1, 3, None).start()

        for way in range(3):
            y_copy(zi, 1, way, y).start()

    def spread(zi, i):
        @pl.when(x > 0)
        def _():
            x_wait(zi, i)
            y_copy(zi, i, 0, y).start()
            y_copy(zi, i, 1, y).start()

    def rows_out(zi):
        for way in range(3):
            y_wait(zi, 1, way)

        @pl.when((x == 1) | (x == 2))
        def _():
            row_copy(zi).start()

    def own_onward(zi):
        y_wait(zi, 0, 0)
        y_onward(zi, 0).start()
        y_wait(zi, 0, 1)

    def onward(zi):
        @pl.when(x > 0)
        def _():
            y_wait(zi, 2, 1)
            y_onward(zi, 2).start()
            y_wait(zi, 2, 0)
            y_wait(zi, 3, 0)
            y_onward(zi, 3).start()
            y_wait(zi, 3, 1)

    def panels_out():
        for d in range(1, 8):
            p_wait(d)
        for d in (1, 2, 3):
            s_copy(d).start()

        @pl.when(bundle < 15)
        def _():
            next_copy().start()

    def attend(slot, keys, values, hide):
        s = lax.dot_general(keys, qs[slot], NT, preferred_element_type=F32)
        s = hide(s)
        before = top[slot]
        now = jnp.maximum(before, jnp.max(s, axis=0, keepdims=True))
        p = jnp.exp2((s - now[:1]) * EXPONENT)
        scale = jnp.exp2((before - now) * EXPONENT)
        top[slot] = now
        tot[slot] = tot[slot] * scale + jnp.sum(p.reshape(-1, 8, COLS), axis=0)
        acc[slot] = acc[slot] * scale[:1] + jnp.dot(
            values.T, p.astype(BF16), preferred_element_type=F32
        )

    def row(kind, plane, zz):
        return kv[kind, pl.ds(at(plane, zz, 0), 4)].reshape(ROW, HEAD)

    token = lax.broadcasted_iota(jnp.int32, (1, COLS), 1) % TOK

    def attend_row(slot, plane, zz):
        offset = jnp.where(slot > 0, TOK * 64, ctx * TOK) - at(plane, zz, 0) * TOK
        key = lax.broadcasted_iota(jnp.int32, (ROW, COLS), 0)

        def hide(s):
            return jnp.where(key <= token + offset, s, HIDDEN)

        attend(slot, row(0, plane, zz), row(1, plane, zz), hide)

    def attend_panels():
        reset(3)
        wait_queries(3, 4)
        for d in (1, 2, 3):
            s_wait(d)
        before = (y == 0) & (bundle > 0)

        @pl.when(before)
        def _():
            for d in range(4):
                next_wait(d)

        def half(which, _):
            block = pan[pl.ds(which * 4, 4)].reshape(32, 16, HEAD).astype(F32)
            keys = block[:, :8].reshape(256, HEAD).astype(BF16)
            values = block[:, 8:].reshape(256, HEAD).astype(BF16)
            here = ctx * TOK + token
            masks = []
            for k in range(4):
                image = slot_image[(bundle - which) * 4 + k]
                reads = (here >= span[image * 2]) & (here < span[image * 2 + 1])
                masks.append(jnp.broadcast_to(jnp.where(reads, 0.0, HIDDEN), (64, COLS)))
            mask = jnp.concatenate(masks, axis=0)
            attend(3, keys, values, lambda s: s + mask)
            return 0

        lax.fori_loop(0, jnp.where(before, 2, 1), half, 0)
        factor = jnp.tanh(jnp.full((1, COLS), gate[0], F32)) / jnp.sum(tot[3], axis=0, keepdims=True)
        for h in range(GROUP):
            c = slice(h * TOK, (h + 1) * TOK)
            cross_out[:, h * HEAD : (h + 1) * HEAD] = (acc[3, :, c] * factor[:, c]).T.astype(BF16)

    for kind in range(2):
        z_copy(kind, 1).start()
        z_copy(kind, 2).start()
    keys_out(0)
    values_out(0)
    for d in range(1, 8):
        p_copy(d).start()
    wait_queries(0, 3)

    @pl.when(x == 3)
    def _():
        q_copy().start()

    pan[y, tp] = staged[tp]
    spread(0, 2)
    spread(0, 3)
    rows_out(0)
    own_onward(0)
    onward(0)
    keys_out(1)
    keys_out(2)

    def ahead(t):
        @pl.when(t == 1)
        def _():
            spread(1, 2)
            spread(2, 2)
            values_out(1)
            values_out(2)

            @pl.when(x == 2)
            def _():
                q_copy().start()

            panels_out()

        @pl.when(t == 2)
        def _():
            keys_out(3)
            for zi in (1, 2):
                spread(zi, 3)
            for zi in (1, 2):
                own_onward(zi)
            for zi in (1, 2):
                rows_out(zi)

        @pl.when(t == 3)
        def _():
            values_out(3)
            onward(1)
            onward(2)

        @pl.when(t == 4)
        def _():
            spread(3, 2)

        @pl.when(t == 5)
        def _():
            spread(3, 3)
            rows_out(3)
            own_onward(3)

        @pl.when(t == 6)
        def _():
            onward(3)

        @pl.when(t == 9)
        def _():
            attend_panels()

    def give_back(slot):
        upper = lax.broadcasted_iota(jnp.int32, (8, COLS), 0) < 4
        total = jnp.sum(tot[slot], axis=0, keepdims=True)
        part_out[slot - 1] = (acc[slot] * (1.0 / total)).astype(BF16)
        stat_out[slot - 1] = jnp.where(upper, top[slot], total)
        for copy in o_copies(slot):
            copy.start()

    def turn(t, code):
        zi, j = code[0] % 4, code[1] % 4
        zz = origin(zi)
        ahead(t)

        @pl.when((x == 0) & (t == 1))
        def _():
            q_wait(2)

        @pl.when((x == 0) & (t == 4))
        def _():
            q_wait(1)

        @pl.when((x > 0) & (j == 0))
        def _():
            y_wait(zi, 0, 2)

        @pl.when((x == 0) & ((t == 0) | (t == 2) | (t == 3) | (t == 7)))
        def _():
            y_wait(zi, 0, 2)

        @pl.when((x > 0) & (j == 1))
        def _():
            y_wait(zi, 2, 2)

        @pl.when(((x == 1) | (x == 2)) & (j == 1))
        def _():
            y_wait(zi, 3, 2)

        @pl.when((x == 3) & (j == 1))
        def _():
            row_wait(zi, 2, 0)

        @pl.when((x == 3) & (j == 2))
        def _():
            y_wait(zi, 3, 2)
            row_wait(zi, 1, 1)

        @pl.when(jnp.where(j == 0, zz <= z, (j == 1) | (x == 0) | (x == 3)))
        def _():
            attend_row(jnp.where(x == 0, j, 0), jnp.where(x == 0, 0, x - j), zz)

        for when, slot in ((7, 2), (8, 1)):

            @pl.when((x == 0) & (t == when))
            def _(slot=slot):
                give_back(slot)

        return code[0] // 4, code[1] // 4

    def digits(values):
        return sum(v * 4**k for k, v in enumerate(values))

    first = [[0, 0, 1, 2, 0, 1, 2, 3, 3, 1, 2, 3], [0, 2, 2, 2, 1, 1, 1, 2, 1, 0, 0, 0]]
    others = [[0, 0, 0, 1, 2, 1, 2, 1, 2, 3, 3, 3], [0, 1, 2, 0, 0, 1, 1, 2, 2, 0, 1, 2]]
    plan = tuple(jnp.where(x == 0, digits(a), digits(b)) for a, b in zip(first, others))
    lax.fori_loop(0, 12, turn, plan)

    @pl.when(x >= 2)
    def _():
        for copy in o_copies(1):
            copy.wait_recv()
        other_top, other_tot = stat_in[0:1], stat_in[4:5]
        own_top = top[0, 0:1]
        both = jnp.maximum(own_top, other_top)
        own = jnp.exp2((own_top - both) * EXPONENT)
        other = other_tot * jnp.exp2((other_top - both) * EXPONENT)
        acc[0] = acc[0] * own + part_in[...].astype(F32) * other
        first = lax.broadcasted_iota(jnp.int32, (8, COLS), 0) == 0
        tot[0] = tot[0] * own + jnp.where(first, other, 0.0)

    inverse = 1.0 / jnp.sum(tot[0], axis=0, keepdims=True)
    for h in range(GROUP):
        c = slice(h * TOK, (h + 1) * TOK)
        self_out[:, h * HEAD : (h + 1) * HEAD] = (acc[0, :, c] * inverse[:, c]).T.astype(BF16)

    for kind in range(2):
        for d in (1, 2):
            z_copy(kind, d).wait_send()
            z_onward(kind, d - 1).wait_send()
    for d in (1, 2, 3):
        s_copy(d).wait_send()
    for d in range(1, 8):
        p_copy(d).wait_send()

    @pl.when(bundle < 15)
    def _():
        next_copy().wait_send()

    def drain(zi, _):
        for i in (0, 1):
            for way in range(3):
                y_copy(zi, i, way, y).wait_send()

        @pl.when(x > 0)
        def _():
            for i in (2, 3):
                for way in range(3):
                    y_copy(zi, i, way, y).wait_send()

        @pl.when(x < 3)
        def _():
            x_copy(zi, 0, 2, None).wait_send()

        @pl.when(x < 2)
        def _():
            x_copy(zi, 1, 3, None).wait_send()

        @pl.when(x == 1)
        def _():
            x_copy(zi, 0, 3, 3).wait_send()

        @pl.when((x == 1) | (x == 2))
        def _():
            row_copy(zi).wait_send()

        return 0

    lax.fori_loop(0, 4, drain, 0)

    @pl.when(x >= 2)
    def _():
        q_copy().wait_send()

    @pl.when(x == 0)
    def _():
        for slot in (1, 2):
            for copy in o_copies(slot):
                copy.wait_send()


def local(query_self, key_value_self, query_cross, panels, image_span, panel_image, cross_gate):
    smem = pl.BlockSpec(memory_space=pltpu.SMEM)
    vmem = pl.BlockSpec(memory_space=pltpu.VMEM)
    hbm = pl.BlockSpec(memory_space=pltpu.HBM)
    dma = pltpu.SemaphoreType.DMA
    shape = jax.ShapeDtypeStruct((TOK, COLS), BF16)
    return pl.pallas_call(
        kernel,
        out_shape=(shape, shape),
        in_specs=[smem] * 3 + [hbm] * 4,
        out_specs=(vmem, vmem),
        scratch_shapes=[
            pltpu.VMEM((4, COLS, HEAD), BF16),
            pltpu.VMEM((2, 64, TOK, HEAD), BF16),
            pltpu.VMEM((8, 16, HEAD), BF16),
            pltpu.VMEM((8, 8, 16, HEAD), BF16),
            pltpu.VMEM((4, HEAD, COLS), F32),
            pltpu.VMEM((4, 8, COLS), F32),
            pltpu.VMEM((4, 8, COLS), F32),
            pltpu.VMEM((2, HEAD, COLS), BF16),
            pltpu.VMEM((HEAD, COLS), BF16),
            pltpu.VMEM((2, 8, COLS), F32),
            pltpu.VMEM((8, COLS), F32),
            dma((4, 2)), dma((4, 2)),
            dma((4, 3)), dma((4, 4)),
            dma((4, 4, 3)), dma((4, 4, 3)),
            dma((4,)), dma((4, 2)),
            dma, dma((3,)),
            dma((2, 2)), dma((2,)),
            dma((8,)), dma((8,)),
            dma((4,)), dma((8,)),
            pltpu.VMEM((2, 1, 8, COLS), BF16), dma((5,)),
        ],
        compiler_params=pltpu.CompilerParams(
            collective_id=0, has_side_effects=True, vmem_limit_bytes=48 << 20
        ),
        name="attention",
    )(image_span.reshape(-1), panel_image, cross_gate, query_self, key_value_self, query_cross, panels)


def solution(mesh):
    return jax.shard_map(
        local,
        mesh=mesh,
        in_specs=(
            P("ctx", "tp"),
            P(None, "ctx", "tp"),
            P("ctx", "tp"),
            P(None, "ctx", "tp", None),
            P(),
            P(),
            P(),
        ),
        out_specs=(P("ctx", "tp"), P("ctx", "tp")),
        check_vma=False,
    )
```

```python
import math

import jax
import jax.numpy as jnp
from jax import lax
from jax.experimental import pallas as pl
from jax.experimental.pallas import tpu as pltpu
from jax.sharding import PartitionSpec as P

MESH = pl.DeviceIdType.MESH
F32 = jnp.float32
BF16 = jnp.bfloat16
HEAD = 128
GROUP = 8
TOK = 128
COLS = GROUP * TOK
ROW = 4 * TOK
START = -1e30
HIDDEN = -1e38
EXPONENT = HEAD**-0.5 * math.log2(math.e)
NT = (((1,), (1,)), ((), ()))
ORIGIN = (0, 3, 1, 2)


def kernel(
    span, slot_image, gate, q_self, kv_own, q_cross, panels, self_out, cross_out,
    qs, kv, staged, pan, acc, top, tot, part_out, part_in, stat_out, stat_in,
    z_send, z_recv, x_send, x_recv, y_send, y_recv, r_send, r_recv,
    q_send, q_recv, o_send, o_recv, p_send, p_recv, s_send, s_recv, panel_in, in_sem,
):
    ctx = lax.axis_index("ctx")
    tp = lax.axis_index("tp")
    x, z, y = ctx // 16, (ctx // 4) % 4, ctx % 4
    bundle = ctx // 4

    def at(xx, zz, yy):
        return xx * 16 + zz * 4 + yy

    def origin(zi):
        if isinstance(zi, int):
            return (z + ORIGIN[zi]) % 4
        return (z + jnp.where(zi == 0, 0, jnp.where(zi == 1, 3, zi - 1))) % 4

    def remote(src, dst, send, recv, where):
        return pltpu.make_async_remote_copy(
            src_ref=src, dst_ref=dst, send_sem=send, recv_sem=recv, device_id=where, device_id_type=MESH
        )

    def reset(slot):
        acc[slot] = jnp.zeros((HEAD, COLS), F32)
        top[slot] = jnp.full((8, COLS), START, F32)
        tot[slot] = jnp.zeros((8, COLS), F32)

    barrier = pltpu.get_barrier_semaphore()
    for d in (1, 2, 3):
        for peer in (at((x + d) % 4, z, y), at(x, (z + d) % 4, y), at(x, z, (y + d) % 4)):
            pl.semaphore_signal(barrier, inc=1, device_id=(peer, tp), device_id_type=MESH)
    for d in range(1, 8):
        pl.semaphore_signal(barrier, inc=1, device_id=(ctx, (tp + d) % 8), device_id_type=MESH)

    @pl.when((y == 0) & (bundle > 0))
    def _():
        for d in range(4):
            pl.semaphore_signal(barrier, inc=1, device_id=(ctx - 4 + d, tp), device_id_type=MESH)

    own_kv = [pltpu.make_async_copy(kv_own.at[k], kv.at[k, ctx], in_sem.at[k]) for k in range(2)]
    own_panel = pltpu.make_async_copy(panels, panel_in, in_sem.at[2])

    def load_queries(array, slot, sem):
        return [
            pltpu.make_async_copy(
                array.at[:, pl.ds(h * HEAD, HEAD)], qs.at[slot, pl.ds(h * TOK, TOK)], in_sem.at[sem]
            )
            for h in range(GROUP)
        ]

    for copy in own_kv + [own_panel] + load_queries(q_self, 0, 3) + load_queries(q_cross, 3, 4):
        copy.start()

    def wait_queries(slot, sem):
        pltpu.make_async_copy(qs.at[slot], qs.at[slot], in_sem.at[sem]).wait()

    reset(0)

    @pl.when(x == 0)
    def _():
        reset(1)
        reset(2)

    own_panel.wait()
    pair = jnp.concatenate([panel_in[0, 0].astype(F32), panel_in[1, 0].astype(F32)], axis=0)
    for h in range(GROUP):
        staged[h] = pair[:, h * HEAD : (h + 1) * HEAD].astype(BF16)

    for copy in own_kv:
        copy.wait()
    pl.semaphore_wait(barrier, jnp.where(bundle < 15, 17, 16))

    def z_copy(kind, zi):
        target = (z + (0, 1, 3)[zi]) % 4
        block = kv.at[kind, ctx]
        return remote(block, block, z_send.at[zi, kind], z_recv.at[zi, kind], (at(x, target, y), tp))

    def z_half(kind, zz, half):
        return kv.at[kind, at(x, zz, y), pl.ds(half * 64, 64)]

    def z_onward(kind, half):
        step = 3 if half == 0 else 1
        block = z_half(kind, (z + step) % 4, half)
        where = (at(x, (z + 4 - step) % 4, y), tp)
        return remote(block, block, z_send.at[3 * half, kind], z_recv.at[3 * half, kind], where)

    def z_wait(kind, zi):
        aside = (ctx, (tp + 1) % 8)
        if zi < 3:
            block = kv.at[kind, at(x, origin(zi), y)]
            remote(block, block, z_send.at[0, 0], z_recv.at[zi, kind], aside).wait_recv()
            return
        for half in range(2):
            block = z_half(kind, origin(3), half)
            remote(block, block, z_send.at[0, 0], z_recv.at[3 * half, kind], aside).wait_recv()

    def item(i):
        return (0, x) if i == 0 else (1, (x, x, x - 1, 1)[i])

    def y_copy(zi, i, way):
        kind, plane = item(i)
        to = (y + (1, 3, 2)[way]) % 4
        block = kv.at[kind, at(plane, origin(zi), y)]
        return remote(block, block, y_send.at[zi, i, way], y_recv.at[zi, i, way], (at(x, z, to), tp))

    def y_wait(zi, i, way):
        kind, plane = item(i)
        yy = (y + (3, 1, 2)[way]) % 4
        block = kv.at[kind, at(plane, origin(zi), yy)]
        remote(block, block, z_send.at[0, 0], y_recv.at[zi, i, way], (ctx, (tp + 1) % 8)).wait_recv()

    def x_copy(zi, i):
        block = kv.at[1, at(x, origin(zi), y)]
        to = (at(x + 1 if i == 2 else 3, z, y), tp)
        return remote(block, block, x_send.at[zi, i - 2], x_recv.at[zi, i - 2], to)

    def x_wait(zi, i):
        kind, plane = item(i)
        block = kv.at[kind, at(plane, origin(zi), y)]
        aside = (ctx, (tp + 1) % 8)
        remote(block, block, z_send.at[0, 0], x_recv.at[zi, i - 2], aside).wait_recv()

    def row_copy(kind, zi, far):
        rows = kv.at[kind, pl.ds(at(x, origin(zi), 0), 4)]
        to = (at(3 if far else x + 1, z, y), tp)
        return remote(rows, rows, r_send.at[kind, zi, far], r_recv.at[kind, zi, far], to)

    def row_wait(kind, zi, far):
        rows = kv.at[kind, pl.ds(at(1 if far else x - 1, origin(zi), 0), 4)]
        aside = (ctx, (tp + 1) % 8)
        remote(rows, rows, z_send.at[0, 0], r_recv.at[kind, zi, far], aside).wait_recv()

    def q_copy():
        return remote(qs.at[0], qs.at[x - 1], q_send, q_recv.at[x - 1], (at(0, z, y), tp))

    def q_wait(slot):
        remote(qs.at[slot], qs.at[slot], q_send, q_recv.at[slot], (ctx, (tp + 1) % 8)).wait_recv()

    def o_copies(slot):
        to = (at(slot + 1, z, y), tp)
        return (
            remote(part_out.at[slot - 1], part_in, o_send.at[slot - 1, 0], o_recv.at[0], to),
            remote(stat_out.at[slot - 1], stat_in, o_send.at[slot - 1, 1], o_recv.at[1], to),
        )

    def p_copy(d):
        to = (tp + d) % 8
        return remote(staged.at[to], pan.at[y, tp], p_send.at[d], p_recv.at[d], (ctx, to))

    def p_wait(d):
        block = pan.at[y, (tp + 8 - d) % 8]
        remote(block, block, p_send.at[0], p_recv.at[d], (ctx, (tp + 1) % 8)).wait_recv()

    def s_copy(d):
        return remote(pan.at[y], pan.at[y], s_send.at[d], s_recv.at[d], (at(x, z, (y + d) % 4), tp))

    def s_wait(d):
        block = pan.at[(y + 4 - d) % 4]
        remote(block, block, s_send.at[d], s_recv.at[d], (ctx, (tp + 1) % 8)).wait_recv()

    def next_copy():
        return remote(pan.at[y], pan.at[4 + y], s_send.at[0], s_recv.at[4 + y], (ctx - y + 4, tp))

    def next_wait(d):
        block = pan.at[4 + d]
        remote(block, block, s_send.at[0], s_recv.at[4 + d], (ctx, (tp + 1) % 8)).wait_recv()

    def block_out(kind, zi):
        if zi > 0:
            z_wait(kind, zi)
        if zi in (1, 2):
            z_onward(kind, zi - 1).start()
        if kind == 1 and zi != 1:

            @pl.when(x < 3)
            def _():
                x_copy(zi, 2).start()

            @pl.when(x == 1)
            def _():
                x_copy(zi, 3).start()

        for way in range(3):
            y_copy(zi, kind, way).start()

    def row_there(kind, zi):
        for way in range(3):
            y_wait(zi, kind, way)

    def rows_out(kind, zi):
        row_there(kind, zi)

        @pl.when(x < 3)
        def _():
            row_copy(kind, zi, 0).start()

        @pl.when(x == 1)
        def _():
            row_copy(kind, zi, 1).start()

    def items():
        return (2, x > 0), (3, x == 3)

    def spread(zi):
        for i, there in items():

            @pl.when(there)
            def _(i=i):
                x_wait(zi, i)
                for way in range(3):
                    y_copy(zi, i, way).start()

    def panels_out():
        for d in range(1, 8):
            p_wait(d)
        for d in (1, 2, 3):
            s_copy(d).start()

        @pl.when(bundle < 15)
        def _():
            next_copy().start()

    def attend(slot, keys, values, hide):
        s = lax.dot_general(keys, qs[slot], NT, preferred_element_type=F32)
        s = hide(s)
        before = top[slot]
        now = jnp.maximum(before, jnp.max(s, axis=0, keepdims=True))
        p = jnp.exp2((s - now[:1]) * EXPONENT)
        scale = jnp.exp2((before - now) * EXPONENT)
        top[slot] = now
        tot[slot] = tot[slot] * scale + jnp.sum(p.reshape(-1, 8, COLS), axis=0)
        acc[slot] = acc[slot] * scale[:1] + jnp.dot(
            values.T, p.astype(BF16), preferred_element_type=F32
        )

    def row(kind, plane, zz):
        return kv[kind, pl.ds(at(plane, zz, 0), 4)].reshape(ROW, HEAD)

    token = lax.broadcasted_iota(jnp.int32, (1, COLS), 1) % TOK

    def attend_rows(slot, rows, causal):
        first = jnp.where(slot > 0, TOK * 64, ctx * TOK)
        key = lax.broadcasted_iota(jnp.int32, (ROW, COLS), 0)

        def hide(s):
            if not causal:
                return s
            parts = []
            for k, (plane, zz) in enumerate(rows):
                seen = key <= token + (first - at(plane, zz, 0) * TOK)
                parts.append(jnp.where(seen, s[k * ROW : (k + 1) * ROW], HIDDEN))
            return jnp.concatenate(parts, axis=0)

        keys, values = [jnp.concatenate([row(k, *r) for r in rows], axis=0) for k in (0, 1)]
        attend(slot, keys, values, hide)

    def attend_panels():
        reset(3)
        wait_queries(3, 4)
        for d in (1, 2, 3):
            s_wait(d)
        before = (y == 0) & (bundle > 0)

        @pl.when(before)
        def _():
            for d in range(4):
                next_wait(d)

        def half(which, _):
            block = pan[pl.ds(which * 4, 4)].reshape(32, 16, HEAD).astype(F32)
            keys = block[:, :8].reshape(256, HEAD).astype(BF16)
            values = block[:, 8:].reshape(256, HEAD).astype(BF16)
            here = ctx * TOK + token
            masks = []
            for k in range(4):
                image = slot_image[(bundle - which) * 4 + k]
                reads = (here >= span[0, image]) & (here < span[1, image])
                masks.append(jnp.broadcast_to(jnp.where(reads, 0.0, HIDDEN), (64, COLS)))
            mask = jnp.concatenate(masks, axis=0)
            attend(3, keys, values, lambda s: s + mask)
            return 0

        lax.fori_loop(0, jnp.where(before, 2, 1), half, 0)
        factor = jnp.tanh(jnp.full((1, COLS), gate[0], F32)) / jnp.sum(tot[3], axis=0, keepdims=True)
        for h in range(GROUP):
            c = slice(h * TOK, (h + 1) * TOK)
            cross_out[:, h * HEAD : (h + 1) * HEAD] = (acc[3, :, c] * factor[:, c]).T.astype(BF16)

    for kind in range(2):
        for zi in (1, 2):
            z_copy(kind, zi).start()
    for kind in range(2):
        block_out(kind, 0)
    for d in range(1, 8):
        p_copy(d).start()
    wait_queries(0, 3)

    @pl.when(x >= 2)
    def _():
        q_copy().start()

    pan[y, tp] = staged[tp]
    rows_out(0, 0)
    spread(0)
    row_there(1, 0)

    def ahead(t):
        @pl.when(t == 1)
        def _():
            for zi in (1, 2):
                block_out(0, zi)

            panels_out()
            for zi in (1, 2):
                block_out(1, zi)
            rows_out(0, 1)
            block_out(0, 3)
            rows_out(0, 2)
            spread(2)

        @pl.when(t == 2)
        def _():
            block_out(1, 3)
            rows_out(1, 1)

        @pl.when(t == 3)
        def _():
            rows_out(0, 3)
            spread(3)

        @pl.when(t == jnp.where(x == 0, 6, 3))
        def _():
            attend_panels()

    def give_back(slot):
        upper = lax.broadcasted_iota(jnp.int32, (8, COLS), 0) < 4
        total = jnp.sum(tot[slot], axis=0, keepdims=True)
        part_out[slot - 1] = (acc[slot] * (1.0 / total)).astype(BF16)
        stat_out[slot - 1] = jnp.where(upper, top[slot], total)
        for copy in o_copies(slot):
            copy.start()

    def first_use(zi, j):
        @pl.when(j == 0)
        def _():
            if zi > 1:
                row_there(1, zi)

        for k, there in ((1, x > 0), (2, x == 3)):

            @pl.when((j == k) & there)
            def _(k=k):
                row_wait(0, zi, k - 1)
                if zi == 1:
                    row_wait(1, zi, k - 1)
                else:
                    for way in range(3):
                        y_wait(zi, k + 1, way)

    def turn(t, code):
        step, zi, j = (c % 8 for c in code)
        ahead(t)

        @pl.when((x == 0) & (t == 1))
        def _():
            q_wait(2)

        @pl.when((x == 0) & (t == 4))
        def _():
            q_wait(1)

        slot = jnp.where(x == 0, j, 0)
        plane = jnp.where(x == 0, 0, x - j)
        both = (step == 3) & (x == 3)
        fresh = (step > 0) & ((x > 0) | (t < 4))
        wait_j = jnp.where(x == 0, 0, j)
        for k in range(4):
            hit = (zi == k) if k in (0, 3) else (zi == k) | (step == 2)

            @pl.when(hit & fresh)
            def _(k=k):
                first_use(k, wait_j)
                pl.when(both)(lambda: first_use(k, 2))

        single, below, above, far = origin(zi), origin(1), origin(2), origin(3)

        @pl.when(((step == 1) & ((j > 0) | (single <= z))) | ((step == 3) & (x < 3)))
        def _():
            attend_rows(slot, ((plane, single),), True)

        @pl.when((step == 2) & (j == 0) & (z > 0))
        def _():
            attend_rows(slot, ((plane, below), (plane, above)), True)

        @pl.when(((step == 2) & (j > 0)) | both | (step == 4))
        def _():
            one = jnp.where(step == 2, below, jnp.where(step == 3, single, z))
            two = jnp.where(step == 2, above, jnp.where(step == 3, single, far))
            attend_rows(slot, ((plane, one), (jnp.where(step == 3, plane - 1, plane), two)), False)

        for when, slot_out in ((3, 2), (5, 1)):

            @pl.when((x == 0) & (t == when))
            def _(slot_out=slot_out):
                give_back(slot_out)

        return tuple(c // 8 for c in code)

    def digits(values):
        return sum(v * 8**k for k, v in enumerate(values))

    first = "11212421", "00131013", "02221100"
    others = "13231330", "00123130", "01010110"
    plan = tuple(
        jnp.where(x == 0, digits(map(int, a)), digits(map(int, b))) for a, b in zip(first, others)
    )
    lax.fori_loop(0, 8, turn, plan)

    @pl.when(x >= 2)
    def _():
        for copy in o_copies(1):
            copy.wait_recv()
        other_top, other_tot = stat_in[0:1], stat_in[4:5]
        own_top = top[0, 0:1]
        both = jnp.maximum(own_top, other_top)
        own = jnp.exp2((own_top - both) * EXPONENT)
        other = other_tot * jnp.exp2((other_top - both) * EXPONENT)
        acc[0] = acc[0] * own + part_in[...].astype(F32) * other
        first = lax.broadcasted_iota(jnp.int32, (8, COLS), 0) == 0
        tot[0] = tot[0] * own + jnp.where(first, other, 0.0)

    inverse = 1.0 / jnp.sum(tot[0], axis=0, keepdims=True)
    for h in range(GROUP):
        c = slice(h * TOK, (h + 1) * TOK)
        self_out[:, h * HEAD : (h + 1) * HEAD] = (acc[0, :, c] * inverse[:, c]).T.astype(BF16)

    for kind in range(2):
        for zi in (1, 2):
            z_copy(kind, zi).wait_send()
            z_onward(kind, zi - 1).wait_send()
    for d in (1, 2, 3):
        s_copy(d).wait_send()
    for d in range(1, 8):
        p_copy(d).wait_send()

    @pl.when(bundle < 15)
    def _():
        next_copy().wait_send()

    for zi in range(4):
        for i in (0, 1):
            for way in range(3):
                y_copy(zi, i, way).wait_send()
        if zi != 1:
            for i, there in items():

                @pl.when(there)
                def _(i=i, zi=zi):
                    for way in range(3):
                        y_copy(zi, i, way).wait_send()

        @pl.when(x < 3)
        def _(zi=zi):
            row_copy(0, zi, 0).wait_send()
            if zi == 1:
                row_copy(1, zi, 0).wait_send()
            else:
                x_copy(zi, 2).wait_send()

        @pl.when(x == 1)
        def _(zi=zi):
            row_copy(0, zi, 1).wait_send()
            if zi == 1:
                row_copy(1, zi, 1).wait_send()
            else:
                x_copy(zi, 3).wait_send()

    @pl.when(x >= 2)
    def _():
        q_copy().wait_send()

    @pl.when(x == 0)
    def _():
        for slot in (1, 2):
            for copy in o_copies(slot):
                copy.wait_send()


def local(query_self, key_value_self, query_cross, panels, image_span, panel_image, cross_gate):
    smem = pl.BlockSpec(memory_space=pltpu.SMEM)
    vmem = pl.BlockSpec(memory_space=pltpu.VMEM)
    hbm = pl.BlockSpec(memory_space=pltpu.HBM)
    dma = pltpu.SemaphoreType.DMA
    shape = jax.ShapeDtypeStruct((TOK, COLS), BF16)
    return pl.pallas_call(
        kernel,
        out_shape=(shape, shape),
        in_specs=[smem] * 3 + [hbm] * 4,
        out_specs=(vmem, vmem),
        scratch_shapes=[
            pltpu.VMEM((4, COLS, HEAD), BF16),
            pltpu.VMEM((2, 64, TOK, HEAD), BF16),
            pltpu.VMEM((8, 16, HEAD), BF16),
            pltpu.VMEM((8, 8, 16, HEAD), BF16),
            pltpu.VMEM((4, HEAD, COLS), F32),
            pltpu.VMEM((4, 8, COLS), F32),
            pltpu.VMEM((4, 8, COLS), F32),
            pltpu.VMEM((2, HEAD, COLS), BF16),
            pltpu.VMEM((HEAD, COLS), BF16),
            pltpu.VMEM((2, 8, COLS), F32),
            pltpu.VMEM((8, COLS), F32),
            dma((4, 2)), dma((4, 2)),
            dma((4, 2)), dma((4, 2)),
            dma((4, 4, 3)), dma((4, 4, 3)),
            dma((2, 4, 2)), dma((2, 4, 2)),
            dma, dma((3,)),
            dma((2, 2)), dma((2,)),
            dma((8,)), dma((8,)),
            dma((4,)), dma((8,)),
            pltpu.VMEM((2, 1, 8, COLS), BF16), dma((5,)),
        ],
        compiler_params=pltpu.CompilerParams(
            collective_id=0, has_side_effects=True, vmem_limit_bytes=64 << 20
        ),
        name="attention",
    )(image_span.T, panel_image, cross_gate, query_self, key_value_self, query_cross, panels)


def solution(mesh):
    return jax.shard_map(
        local,
        mesh=mesh,
        in_specs=(
            P("ctx", "tp"),
            P(None, "ctx", "tp"),
            P("ctx", "tp"),
            P(None, "ctx", "tp", None),
            P(),
            P(),
            P(),
        ),
        out_specs=(P("ctx", "tp"), P("ctx", "tp")),
        check_vma=False,
    )
```

```python
import math

import jax
import jax.numpy as jnp
from jax import lax
from jax.experimental import pallas as pl
from jax.experimental.pallas import tpu as pltpu
from jax.sharding import PartitionSpec as P

MESH = pl.DeviceIdType.MESH
F32 = jnp.float32
BF16 = jnp.bfloat16
HEAD = 128
GROUP = 8
TOK = 128
COLS = GROUP * TOK
ROW = 4 * TOK
START = -1e30
HIDDEN = -1e38
EXPONENT = HEAD**-0.5 * math.log2(math.e)
NT = (((1,), (1,)), ((), ()))
ORIGIN = (0, 3, 1, 2)


def kernel(
    span, slot_image, gate, q_self, kv_own, q_cross, panels, self_out, cross_out,
    qs, kv, staged, pan, acc, top, tot, part_out, part_in, stat_out, stat_in,
    z_send, z_recv, x_send, x_recv, y_send, y_recv, r_send, r_recv,
    q_send, q_recv, o_send, o_recv, p_send, p_recv, s_send, s_recv, panel_in, in_sem, result, out_sem,
):
    ctx = lax.axis_index("ctx")
    tp = lax.axis_index("tp")
    x, z, y = ctx // 16, (ctx // 4) % 4, ctx % 4
    bundle = ctx // 4

    def at(xx, zz, yy):
        return xx * 16 + zz * 4 + yy

    def origin(zi):
        if isinstance(zi, int):
            return (z + ORIGIN[zi]) % 4
        return (z + jnp.where(zi == 0, 0, jnp.where(zi == 1, 3, zi - 1))) % 4

    def remote(src, dst, send, recv, where):
        return pltpu.make_async_remote_copy(
            src_ref=src, dst_ref=dst, send_sem=send, recv_sem=recv, device_id=where, device_id_type=MESH
        )

    def reset(slot):
        acc[slot] = jnp.zeros((HEAD, COLS), F32)
        top[slot] = jnp.full((8, COLS), START, F32)
        tot[slot] = jnp.zeros((8, COLS), F32)

    barrier = pltpu.get_barrier_semaphore()
    for d in (1, 2, 3):
        for peer in (at((x + d) % 4, z, y), at(x, (z + d) % 4, y), at(x, z, (y + d) % 4)):
            pl.semaphore_signal(barrier, inc=1, device_id=(peer, tp), device_id_type=MESH)
    for d in range(1, 8):
        pl.semaphore_signal(barrier, inc=1, device_id=(ctx, (tp + d) % 8), device_id_type=MESH)

    @pl.when((y == 0) & (bundle > 0))
    def _():
        for d in range(4):
            pl.semaphore_signal(barrier, inc=1, device_id=(ctx - 4 + d, tp), device_id_type=MESH)

    own_kv = [pltpu.make_async_copy(kv_own.at[k], kv.at[k, ctx], in_sem.at[k]) for k in range(2)]
    own_panel = pltpu.make_async_copy(panels, panel_in, in_sem.at[2])

    def load_queries(array, slot, sem):
        return [
            pltpu.make_async_copy(
                array.at[:, pl.ds(h * HEAD, HEAD)], qs.at[slot, pl.ds(h * TOK, TOK)], in_sem.at[sem]
            )
            for h in range(GROUP)
        ]

    for copy in own_kv + [own_panel] + load_queries(q_self, 0, 3) + load_queries(q_cross, 3, 4):
        copy.start()

    def wait_queries(slot, sem):
        pltpu.make_async_copy(qs.at[slot], qs.at[slot], in_sem.at[sem]).wait()

    for copy in own_kv:
        copy.wait()
    pl.semaphore_wait(barrier, jnp.where(bundle < 15, 17, 16))

    def z_copy(kind, zi):
        target = (z + (0, 1, 3)[zi]) % 4
        block = kv.at[kind, ctx]
        return remote(block, block, z_send.at[zi, kind], z_recv.at[zi, kind], (at(x, target, y), tp))

    def z_half(kind, zz, half):
        return kv.at[kind, at(x, zz, y), pl.ds(half * 64, 64)]

    def z_onward(kind, half):
        step = 3 if half == 0 else 1
        block = z_half(kind, (z + step) % 4, half)
        where = (at(x, (z + 4 - step) % 4, y), tp)
        return remote(block, block, z_send.at[3 * half, kind], z_recv.at[3 * half, kind], where)

    def z_wait(kind, zi):
        aside = (ctx, (tp + 1) % 8)
        if zi < 3:
            block = kv.at[kind, at(x, origin(zi), y)]
            remote(block, block, z_send.at[0, 0], z_recv.at[zi, kind], aside).wait_recv()
            return
        for half in range(2):
            block = z_half(kind, origin(3), half)
            remote(block, block, z_send.at[0, 0], z_recv.at[3 * half, kind], aside).wait_recv()

    def item(i):
        return (i, x) if i < 2 else (1, x + 1 - i)

    def senders(far):
        return x == 1 if far else x < 3

    def receivers(far):
        return x == 3 if far else x > 0

    def rows_over(kind, zi, plane, far):
        return True if kind == 0 else (plane == 3) & (far == 0 and zi in (1, 2))

    def y_copy(zi, i, way):
        kind, plane = item(i)
        to = (y + (1, 3, 2)[way]) % 4
        block = kv.at[kind, at(plane, origin(zi), y)]
        return remote(block, block, y_send.at[zi, i, way], y_recv.at[zi, i, way], (at(x, z, to), tp))

    def y_wait(zi, i, way):
        kind, plane = item(i)
        yy = (y + (3, 1, 2)[way]) % 4
        block = kv.at[kind, at(plane, origin(zi), yy)]
        remote(block, block, z_send.at[0, 0], y_recv.at[zi, i, way], (ctx, (tp + 1) % 8)).wait_recv()

    def x_copy(zi, far):
        block = kv.at[1, at(x, origin(zi), y)]
        to = (at(x + 1 + far, z, y), tp)
        return remote(block, block, x_send.at[zi, far], x_recv.at[zi, far], to)

    def x_wait(zi, i):
        kind, plane = item(i)
        block = kv.at[kind, at(plane, origin(zi), y)]
        aside = (ctx, (tp + 1) % 8)
        remote(block, block, z_send.at[0, 0], x_recv.at[zi, i - 2], aside).wait_recv()

    def row_copy(kind, zi, far):
        rows = kv.at[kind, pl.ds(at(x, origin(zi), 0), 4)]
        to = (at(x + 1 + far, z, y), tp)
        return remote(rows, rows, r_send.at[kind, zi, far], r_recv.at[kind, zi, far], to)

    def row_wait(kind, zi, far):
        rows = kv.at[kind, pl.ds(at(x - 1 - far, origin(zi), 0), 4)]
        aside = (ctx, (tp + 1) % 8)
        remote(rows, rows, z_send.at[0, 0], r_recv.at[kind, zi, far], aside).wait_recv()

    def q_copy():
        return remote(qs.at[0], qs.at[x - 1], q_send, q_recv.at[x - 1], (at(0, z, y), tp))

    def q_wait(slot):
        remote(qs.at[slot], qs.at[slot], q_send, q_recv.at[slot], (ctx, (tp + 1) % 8)).wait_recv()

    def o_copies(slot):
        to = (at(slot + 1, z, y), tp)
        return (
            remote(part_out.at[slot - 1], part_in, o_send.at[slot - 1, 0], o_recv.at[0], to),
            remote(stat_out.at[slot - 1], stat_in, o_send.at[slot - 1, 1], o_recv.at[1], to),
        )

    def p_copy(d):
        to = (tp + d) % 8
        return remote(staged.at[to], pan.at[y, tp], p_send.at[d], p_recv.at[d], (ctx, to))

    def p_wait(d):
        block = pan.at[y, (tp + 8 - d) % 8]
        remote(block, block, p_send.at[0], p_recv.at[d], (ctx, (tp + 1) % 8)).wait_recv()

    def s_copy(d):
        return remote(pan.at[y], pan.at[y], s_send.at[d], s_recv.at[d], (at(x, z, (y + d) % 4), tp))

    def s_wait(d):
        block = pan.at[(y + 4 - d) % 4]
        remote(block, block, s_send.at[d], s_recv.at[d], (ctx, (tp + 1) % 8)).wait_recv()

    def next_copy():
        return remote(pan.at[y], pan.at[4 + y], s_send.at[0], s_recv.at[4 + y], (ctx - y + 4, tp))

    def next_wait(d):
        block = pan.at[4 + d]
        remote(block, block, s_send.at[0], s_recv.at[4 + d], (ctx, (tp + 1) % 8)).wait_recv()

    def block_out(kind, zi):
        if zi > 0:
            z_wait(kind, zi)
        if zi in (1, 2):
            z_onward(kind, zi - 1).start()
        if kind == 1:
            for far in range(2):
                pl.when(senders(far) & ~rows_over(1, zi, x + 1 + far, far))(x_copy(zi, far).start)

        for way in range(3):
            y_copy(zi, kind, way).start()

    def row_there(kind, zi):
        for way in range(3):
            y_wait(zi, kind, way)

    def rows_out(kind, zi):
        row_there(kind, zi)
        for far in range(2):
            pl.when(senders(far) & rows_over(kind, zi, x + 1 + far, far))(row_copy(kind, zi, far).start)

    def spread(zi):
        for far in range(2):

            @pl.when(receivers(far) & ~rows_over(1, zi, x, far))
            def _(i=far + 2):
                x_wait(zi, i)
                for way in range(3):
                    y_copy(zi, i, way).start()

    def panels_out():
        for d in range(1, 8):
            p_wait(d)
        for d in (1, 2, 3):
            s_copy(d).start()

        @pl.when(bundle < 15)
        def _():
            next_copy().start()

    def sent(zi):
        for i in (0, 1):
            for way in range(3):
                y_copy(zi, i, way).wait_send()
        for far in range(2):

            @pl.when(senders(far))
            def _(far=far):
                row_copy(0, zi, far).wait_send()
                over = rows_over(1, zi, x + 1 + far, far)
                pl.when(over)(lambda: row_copy(1, zi, far).wait_send())
                pl.when(~over)(lambda: x_copy(zi, far).wait_send())

            @pl.when(receivers(far) & ~rows_over(1, zi, x, far))
            def _(i=far + 2):
                for way in range(3):
                    y_copy(zi, i, way).wait_send()

    def sent_early():
        for kind in range(2):
            for zi in (1, 2):
                z_copy(kind, zi).wait_send()
                z_onward(kind, zi - 1).wait_send()
        for d in (1, 2, 3):
            s_copy(d).wait_send()
        for d in range(1, 8):
            p_copy(d).wait_send()
        pl.when(bundle < 15)(lambda: next_copy().wait_send())
        pl.when(x >= 2)(lambda: q_copy().wait_send())
        for zi in (0, 1, 2):
            sent(zi)

    def attend(slot, keys, values, hide):
        s = lax.dot_general(keys, qs[slot], NT, preferred_element_type=F32)
        s = hide(s)
        before = top[slot]
        now = jnp.maximum(before, jnp.max(s, axis=0, keepdims=True))
        p = jnp.exp2((s - now[:1]) * EXPONENT)
        scale = jnp.exp2((before - now) * EXPONENT)
        top[slot] = now
        tot[slot] = tot[slot] * scale + jnp.sum(p.reshape(-1, 8, COLS), axis=0)
        acc[slot] = acc[slot] * scale[:1] + jnp.dot(
            values.T, p.astype(BF16), preferred_element_type=F32
        )

    def row(kind, plane, zz):
        return kv[kind, pl.ds(at(plane, zz, 0), 4)].reshape(ROW, HEAD)

    token = lax.broadcasted_iota(jnp.int32, (1, COLS), 1) % TOK

    def attend_rows(slot, rows, causal):
        first = jnp.where(slot > 0, TOK * 64, ctx * TOK)
        key = lax.broadcasted_iota(jnp.int32, (ROW, COLS), 0)

        def hide(s):
            if not causal:
                return s
            parts = []
            for k, (plane, zz) in enumerate(rows):
                seen = key <= token + (first - at(plane, zz, 0) * TOK)
                parts.append(jnp.where(seen, s[k * ROW : (k + 1) * ROW], HIDDEN))
            return jnp.concatenate(parts, axis=0)

        keys, values = [jnp.concatenate([row(k, *r) for r in rows], axis=0) for k in (0, 1)]
        attend(slot, keys, values, hide)

    def out_copy(which, h):
        c = pl.ds(h * HEAD, HEAD)
        out = (self_out, cross_out)[which]
        return pltpu.make_async_copy(result.at[which, :, c], out.at[:, c], out_sem.at[which, h])

    def attend_panels():
        reset(3)
        wait_queries(3, 4)
        for d in (1, 2, 3):
            s_wait(d)
        before = (y == 0) & (bundle > 0)

        @pl.when(before)
        def _():
            for d in range(4):
                next_wait(d)

        def half(which, _):
            block = pan[pl.ds(which * 4, 4)].reshape(32, 16, HEAD).astype(F32)
            keys = block[:, :8].reshape(256, HEAD).astype(BF16)
            values = block[:, 8:].reshape(256, HEAD).astype(BF16)
            here = ctx * TOK + token
            masks = []
            for k in range(4):
                image = slot_image[(bundle - which) * 4 + k]
                reads = (here >= span[0, image]) & (here < span[1, image])
                masks.append(jnp.broadcast_to(jnp.where(reads, 0.0, HIDDEN), (64, COLS)))
            mask = jnp.concatenate(masks, axis=0)
            attend(3, keys, values, lambda s: s + mask)
            return 0

        lax.fori_loop(0, jnp.where(before, 2, 1), half, 0)
        factor = jnp.tanh(jnp.full((1, COLS), gate[0], F32)) / jnp.sum(tot[3], axis=0, keepdims=True)
        for h in range(GROUP):
            c = slice(h * TOK, (h + 1) * TOK)
            result[1, :, c] = (acc[3, :, c] * factor[:, c]).T.astype(BF16)
            out_copy(1, h).start()

    for kind in range(2):
        for zi in (1, 2):
            z_copy(kind, zi).start()
    for kind in range(2):
        block_out(kind, 0)
    own_panel.wait()
    pair = jnp.concatenate([panel_in[0, 0].astype(F32), panel_in[1, 0].astype(F32)], axis=0)
    for h in range(GROUP):
        staged[h] = pair[:, h * HEAD : (h + 1) * HEAD].astype(BF16)

    for d in range(1, 8):
        p_copy(d).start()
    wait_queries(0, 3)

    @pl.when(x >= 2)
    def _():
        q_copy().start()

    reset(0)

    @pl.when(x == 0)
    def _():
        reset(1)
        reset(2)

    pan[y, tp] = staged[tp]
    rows_out(0, 0)
    spread(0)
    row_there(1, 0)

    def ahead(t):
        @pl.when(t == 1)
        def _():
            for zi in (1, 2):
                block_out(0, zi)

            for zi in (1, 2):
                block_out(1, zi)
            panels_out()
            rows_out(0, 1)
            block_out(0, 3)
            rows_out(0, 2)
            spread(1)
            spread(2)

        @pl.when(t == 2)
        def _():
            block_out(1, 3)
            rows_out(1, 1)
            rows_out(1, 2)

        @pl.when(t == 3)
        def _():
            rows_out(0, 3)
            spread(3)

        pl.when(t == jnp.where(x == 0, 8, 6))(sent_early)

        @pl.when(t == jnp.where(x == 0, 7, 3))
        def _():
            attend_panels()

    def give_back(slot):
        upper = lax.broadcasted_iota(jnp.int32, (8, COLS), 0) < 4
        total = jnp.sum(tot[slot], axis=0, keepdims=True)
        part_out[slot - 1] = (acc[slot] * (1.0 / total)).astype(BF16)
        stat_out[slot - 1] = jnp.where(upper, top[slot], total)
        for copy in o_copies(slot):
            copy.start()

    def first_use(zi, j):
        @pl.when(j == 0)
        def _():
            if zi == 3:
                row_there(1, 3)

        for k in range(1, 3):

            @pl.when((j == k) & receivers(k - 1))
            def _(k=k):
                row_wait(0, zi, k - 1)
                pl.when(rows_over(1, zi, x, k - 1))(lambda: row_wait(1, zi, k - 1))

                @pl.when(~rows_over(1, zi, x, k - 1))
                def _():
                    for way in range(3):
                        y_wait(zi, k + 1, way)

    def turn(t, code):
        step, zi, j = (c % 8 for c in code)
        ahead(t)

        @pl.when((x == 0) & (t == 1))
        def _():
            q_wait(2)

        @pl.when((x == 0) & (t == 3))
        def _():
            q_wait(1)

        slot = jnp.where(x == 0, j, 0)
        plane = jnp.where(x == 0, 0, x - j)
        both = (step == 3) & (x == 3)
        fresh = (step > 0) & ((x > 0) | (t == 2) | (t == 5))
        wait_j = jnp.where(x == 0, 0, j)
        for k in range(4):
            hit = (zi == k) if k in (0, 3) else (zi == k) | (step == 2)

            @pl.when(hit & fresh)
            def _(k=k):
                first_use(k, wait_j)
                pl.when(both)(lambda: first_use(k, 2))

        single, below, above = origin(zi), origin(1), origin(2)

        @pl.when(((step == 1) & ((j > 0) | (single <= z))) | ((step == 3) & ~both))
        def _():
            attend_rows(slot, ((plane, single),), True)

        @pl.when((step == 2) & (j == 0) & (z > 0))
        def _():
            attend_rows(slot, ((plane, below), (plane, above)), True)

        @pl.when(((step == 2) & (j > 0)) | both)
        def _():
            one = jnp.where(step == 2, below, single)
            two = jnp.where(step == 2, above, single)
            attend_rows(slot, ((plane, one), (jnp.where(step == 3, plane - 1, plane), two)), False)

        for when, slot_out in ((5, 2), (6, 1)):

            @pl.when((x == 0) & (t == when))
            def _(slot_out=slot_out):
                give_back(slot_out)

        return tuple(c // 8 for c in code)

    def digits(values):
        return sum(v * 8**k for k, v in enumerate(values))

    first = "112211121", "001103313", "022112100"
    others = "132313300", "001231300", "010101100"
    plan = tuple(
        jnp.where(x == 0, digits(map(int, a)), digits(map(int, b))) for a, b in zip(first, others)
    )
    lax.fori_loop(0, 9, turn, plan)

    @pl.when(x >= 2)
    def _():
        for copy in o_copies(1):
            copy.wait_recv()
        other_top, other_tot = stat_in[0:1], stat_in[4:5]
        own_top = top[0, 0:1]
        both = jnp.maximum(own_top, other_top)
        own = jnp.exp2((own_top - both) * EXPONENT)
        other = other_tot * jnp.exp2((other_top - both) * EXPONENT)
        acc[0] = acc[0] * own + part_in[...].astype(F32) * other
        first = lax.broadcasted_iota(jnp.int32, (8, COLS), 0) == 0
        tot[0] = tot[0] * own + jnp.where(first, other, 0.0)

    inverse = 1.0 / jnp.sum(tot[0], axis=0, keepdims=True)
    for h in range(GROUP):
        c = slice(h * TOK, (h + 1) * TOK)
        result[0, :, c] = (acc[0, :, c] * inverse[:, c]).T.astype(BF16)
        out_copy(0, h).start()

    sent(3)

    @pl.when(x == 0)
    def _():
        for slot in (1, 2):
            for copy in o_copies(slot):
                copy.wait_send()

    for which in range(2):
        for h in range(GROUP):
            out_copy(which, h).wait()


def local(query_self, key_value_self, query_cross, panels, image_span, panel_image, cross_gate):
    smem = pl.BlockSpec(memory_space=pltpu.SMEM)
    hbm = pl.BlockSpec(memory_space=pltpu.HBM)
    dma = pltpu.SemaphoreType.DMA
    shape = jax.ShapeDtypeStruct((TOK, COLS), BF16)
    return pl.pallas_call(
        kernel,
        out_shape=(shape, shape),
        in_specs=[smem] * 3 + [hbm] * 4,
        out_specs=(hbm, hbm),
        scratch_shapes=[
            pltpu.VMEM((4, COLS, HEAD), BF16),
            pltpu.VMEM((2, 64, TOK, HEAD), BF16),
            pltpu.VMEM((8, 16, HEAD), BF16),
            pltpu.VMEM((8, 8, 16, HEAD), BF16),
            pltpu.VMEM((4, HEAD, COLS), F32),
            pltpu.VMEM((4, 8, COLS), F32),
            pltpu.VMEM((4, 8, COLS), F32),
            pltpu.VMEM((2, HEAD, COLS), BF16),
            pltpu.VMEM((HEAD, COLS), BF16),
            pltpu.VMEM((2, 8, COLS), F32),
            pltpu.VMEM((8, COLS), F32),
            dma((4, 2)), dma((4, 2)),
            dma((4, 3)), dma((4, 3)),
            dma((4, 5, 3)), dma((4, 5, 3)),
            dma((2, 4, 3)), dma((2, 4, 3)),
            dma, dma((3,)),
            dma((2, 2)), dma((2,)),
            dma((8,)), dma((8,)),
            dma((4,)), dma((8,)),
            pltpu.VMEM((2, 1, 8, COLS), BF16), dma((5,)),
            pltpu.VMEM((2, TOK, COLS), BF16), dma((2, GROUP)),
        ],
        compiler_params=pltpu.CompilerParams(
            collective_id=0, has_side_effects=True, vmem_limit_bytes=64 << 20
        ),
        name="attention",
    )(image_span.T, panel_image, cross_gate, query_self, key_value_self, query_cross, panels)


def solution(mesh):
    return jax.shard_map(
        local,
        mesh=mesh,
        in_specs=(
            P("ctx", "tp"),
            P(None, "ctx", "tp"),
            P("ctx", "tp"),
            P(None, "ctx", "tp", None),
            P(),
            P(),
            P(),
        ),
        out_specs=(P("ctx", "tp"), P("ctx", "tp")),
        check_vma=False,
    )
```
